32 devices in a mesh: dp: 8 (over z, x), expert: 4 (over y, core).
Axes of the slice: x: 2, y: 2, z: 4, core: 2. Of those that a mesh axis runs over, the one named last changes fastest.
Arguments:
- tokens: bfloat16 [64, 197, 768], P(('dp', 'expert')), may hold values from -6 to 6
- route_ids: int32 [64, 197, 2], P(('dp', 'expert')), may hold values from 0 to 3, all different within a row; in each aligned block of 394 rows (0 to 393, 394 to 787, ..., all dimensions but the last counted through in order) at most 295 rows name the same one
- cotangent: bfloat16 [64, 197, 768], P(('dp', 'expert')), may hold values from -6 to 6
- norm1_gain: float32 [768], replicated, may hold values from 0.5 to 1.5
- norm1_shift: float32 [768], replicated, may hold values from -1 to 1
- qkv_weight: bfloat16 [768, 2304], replicated, may hold values from -0.21875 to 0.21875
- qv_bias: float32 [2, 768], replicated, may hold values from -1 to 1
- out_weight: bfloat16 [768, 768], replicated, may hold values from -1.5 to 1.5
- out_bias: float32 [768], replicated, may hold values from -1 to 1
- norm2_gain: float32 [768], replicated, may hold values from 0.5 to 1.5
- norm2_shift: float32 [768], replicated, may hold values from -1 to 1
- router_weight: bfloat16 [768, 4], replicated, may hold values from -0.15625 to 0.15625
- expert_in: bfloat16 [4, 768, 3072], P('expert'), may hold values from -0.21875 to 0.21875
- expert_in_bias: float32 [4, 3072], P('expert'), may hold values from -1 to 1
- expert_out: bfloat16 [4, 3072, 768], P('expert'), may hold values from -0.4375 to 0.4375
- expert_out_bias: float32 [4, 768], P('expert'), may hold values from -2 to 2
Outputs:
- output: bfloat16 [64, 197, 768], P(('dp', 'expert'))
- grad_tokens: float32 [64, 197, 768], P(('dp', 'expert'))
- grad_norm1_gain: float32 [768], replicated
- grad_norm1_shift: float32 [768], replicated
- grad_qkv_weight: float32 [768, 2304], replicated
- grad_qv_bias: float32 [2, 768], replicated
- grad_out_weight: float32 [768, 768], replicated
- grad_out_bias: float32 [768], replicated
- grad_norm2_gain: float32 [768], replicated
- grad_norm2_shift: float32 [768], replicated
- grad_router_weight: float32 [768, 4], replicated
- grad_expert_in: float32 [4, 768, 3072], P('expert', None, 'dp')
- grad_expert_in_bias: float32 [4, 3072], P('expert', 'dp')
- grad_expert_out: float32 [4, 3072, 768], P('expert', 'dp')
- grad_expert_out_bias: float32 [4, 768], P('expert', 'dp')
The draws below stay inside these ranges and needn't reach their ends.
Inputs may be any that keep to these rules, and one draw needn't show every extreme that they name: `route_ids`: each token names two different experts. Among the tokens of one device no expert is named more than 295 times, and in every draw some expert is named exactly 295 times by the tokens of some device.
All inputs are finite; a program needn't handle non-finite values.
Results may differ from the reference program's by a relative error of at most 0.02.
Values may be sent and summed in bfloat16 or wider, within the bound.
A program may use at most 192 MiB of HBM per device.

```python
import math
from functools import partial
import jax
import jax.numpy as jnp
import numpy as np
from jax import lax

D = 768
HEADS = 12
HEAD = 64
FF = 3072
SEQ = 197
IMG_DEV = 2
EXPERTS = 4
TOK_DEV = 394
IMAGES = 64
CAP = 295


def block_levels(own_key, extent, split, smallest, high):
    def one(axis_at, blocks):
        draws = jax.random.uniform(jax.random.fold_in(jax.random.fold_in(own_key, 6), axis_at), (blocks,), jnp.float32, smallest / len(split), high / len(split))
        return jnp.repeat(jnp.exp(draws), extent[axis_at] // blocks).reshape((-1,) + (1,) * (len(extent) - axis_at - 1))

    level = one(*split[0])
    for cut in split[1:]:
        level = level * one(*cut)
    return level


def assign_block(own_key, own, number, rows, amount, top, bound, skew):
    sequence = jax.random.permutation(own_key, amount)
    packed, common = portions_of(amount, rows * top, bound, skew, True), portions_of(amount, rows * top, bound, skew, False)
    places = jnp.arange(amount)

    def named(lengths, turn):
        used = int((lengths > 0).sum())
        fixed = max(1, used // 4)
        passed = fixed + (places - fixed + turn * (used - fixed)) % max(1, amount - fixed)
        return jnp.zeros((amount,), jnp.int32).at[sequence[jnp.where(places < fixed, places, passed)]].set(jnp.asarray(lengths, jnp.int32))

    lengths = jnp.where(number % 4 == 0, named(packed, number // 4), named(common, number - number // 4 - 1))
    mixed = jax.random.permutation(jax.random.fold_in(own, 3), amount)
    giver, sink = mixed[0:amount // 2 * 2:2], mixed[1:amount // 2 * 2:2]
    room = jnp.minimum(lengths[giver] - 1, bound - lengths[sink]) // 2
    room = jnp.where((giver == sequence[0]) | (sink == sequence[0]) | (lengths[sink] == 0), 0, jnp.maximum(room, 0))
    passed = jax.random.randint(jax.random.fold_in(own, 4), (amount // 2,), 0, 1 << 20) % (room + 1)
    lengths = lengths.at[giver].add(-passed).at[sink].add(passed)
    items = jnp.searchsorted(jnp.cumsum(lengths), jnp.arange(rows * top), side="right").astype(jnp.int32)
    table = items.reshape(top, rows).T
    table = table[jax.random.permutation(jax.random.fold_in(own, 1), rows)]
    turn = jax.random.randint(jax.random.fold_in(own, 2), (rows, 1), 0, top)
    return jnp.take_along_axis(table, (jnp.arange(top)[None, :] + turn) % top, axis=1)


def portions_of(number_of, total, bound, slope, full):
    loads = [(1 << 20) // math.isqrt(standing ** slope) + 1 for standing in range(1, number_of + 1)]
    largest = bound if full else min(bound, max(-(-total // number_of), total * loads[0] // sum(loads)))
    least = 1 if total - largest >= number_of - 1 else 0
    counts, spare = [largest] + [least] * (number_of - 1), total - largest - least * (number_of - 1)
    while spare > 0:
        free = [i for i in range(1, number_of) if counts[i] < largest] or [i for i in range(1, number_of) if counts[i] < bound]
        mass, remaining = sum([loads[i] for i in free]), spare
        for i in free:
            extra = min(bound - counts[i], max(1, remaining * loads[i] // mass), spare)
            counts[i] = counts[i] + extra
            spare = spare - extra
    return np.array(counts)


def scatter_about(own_key, shape, deviation, limit, shards=(), kind=jnp.bfloat16):
    entries = deviation * jax.random.normal(own_key, shape, jnp.float32)
    if shards:
        entries = entries * block_levels(own_key, shape, shards, -0.22, 0.18)
    return jnp.clip(entries, -limit, limit).astype(kind)


def setup_inputs(seed: int = 0) -> dict:
    streams_of = jax.random.split(jax.random.key(seed), 17)
    tokens = scatter_about(streams_of[0], (IMAGES, SEQ, D), 1.0, 6.0, ((0, 32),))
    route_ids_keys = jax.random.split(jax.random.fold_in(streams_of[1], 1), IMAGES * SEQ // TOK_DEV)
    route_ids_turns = jax.random.permutation(jax.random.fold_in(streams_of[1], 3), IMAGES * SEQ // TOK_DEV)
    route_ids = jax.vmap(lambda own, number: assign_block(jax.random.fold_in(streams_of[1], 2), own, number, TOK_DEV, EXPERTS, 2, CAP, 2))(route_ids_keys, route_ids_turns).reshape((IMAGES, SEQ, 2))
    cotangent = scatter_about(streams_of[2], (IMAGES, SEQ, D), 1.0, 6.0, ((0, 32),))
    norm1_gain = jnp.clip(1.0 + 0.1 * jax.random.normal(streams_of[3], (D,), jnp.float32), 0.5, 1.5)
    norm1_shift = scatter_about(streams_of[4], (D,), 0.2, 1.0, (), jnp.float32)
    qkv_weight = scatter_about(streams_of[5], (D, 3 * D), D ** -0.5, 0.21875)
    qv_bias = scatter_about(streams_of[6], (2, D), 0.2, 1.0, (), jnp.float32)
    out_weight = scatter_about(streams_of[7], (D, D), (D * 4 // SEQ) ** -0.5, 1.5)
    out_bias = scatter_about(streams_of[8], (D,), 0.2, 1.0, (), jnp.float32)
    norm2_gain = jnp.clip(1.0 + 0.1 * jax.random.normal(streams_of[9], (D,), jnp.float32), 0.5, 1.5)
    norm2_shift = scatter_about(streams_of[10], (D,), 0.2, 1.0, (), jnp.float32)
    router_weight = scatter_about(streams_of[11], (D, EXPERTS), (2 * D) ** -0.5, 0.15625)
    expert_in = scatter_about(streams_of[12], (EXPERTS, D, FF), D ** -0.5, 0.21875, ((0, 4),))
    expert_in_bias = scatter_about(streams_of[13], (EXPERTS, FF), 0.2, 1.0, ((0, 4),), jnp.float32)
    expert_out = scatter_about(streams_of[14], (EXPERTS, FF, D), (FF // (EXPERTS * EXPERTS)) ** -0.5, 0.4375, ((0, 4),))
    expert_out_bias = scatter_about(streams_of[15], (EXPERTS, D), (0.1 * EXPERTS), 2.0, ((0, 4),), jnp.float32)
    return {"tokens": tokens, "route_ids": route_ids, "cotangent": cotangent, "norm1_gain": norm1_gain, "norm1_shift": norm1_shift, "qkv_weight": qkv_weight, "qv_bias": qv_bias, "out_weight": out_weight, "out_bias": out_bias, "norm2_gain": norm2_gain, "norm2_shift": norm2_shift, "router_weight": router_weight, "expert_in": expert_in, "expert_in_bias": expert_in_bias, "expert_out": expert_out, "expert_out_bias": expert_out_bias}


highest = lax.Precision.HIGHEST
epsilon = 1e-06

@jax.custom_vjp
def low(v):
    return lax.optimization_barrier(v.astype(jnp.bfloat16)).astype(jnp.float32)

@jax.custom_vjp
def low_back(v):
    return v

def low_keep(v):
    return (low(v), None)

def low_pass(kept, grad):
    return (grad,)

def back_keep(v):
    return (v, None)

def back_low(kept, grad):
    return (low(grad),)
low.defvjp(low_keep, low_pass)
low_back.defvjp(back_keep, back_low)

def norm_rows(values, gain, shift):
    mean_row = lax.optimization_barrier(jnp.mean(values, axis=-1, keepdims=True))
    centred = values - mean_row
    variance = lax.optimization_barrier(jnp.mean(centred * centred, axis=-1, keepdims=True))
    return centred * lax.rsqrt(variance + epsilon) * gain + shift

def attend(one_image, norm1_gain, norm1_shift, qkv_weight, bias_row, out_weight, out_bias):
    hidden1 = low(norm_rows(one_image, norm1_gain, norm1_shift))
    qkv_rows = low_back(low(jnp.dot(hidden1, qkv_weight, precision=highest) + bias_row))
    query_rows = qkv_rows[:, :D].reshape(SEQ, HEADS, HEAD)
    key_rows = qkv_rows[:, D:2 * D].reshape(SEQ, HEADS, HEAD)
    value_rows = qkv_rows[:, 2 * D:].reshape(SEQ, HEADS, HEAD)
    scores = low_back(jnp.einsum('qhd,khd->hqk', query_rows, key_rows, precision=highest) * (1.0 / HEAD ** 0.5))
    attn_probs = low(jax.nn.softmax(scores, axis=-1))
    mixed_rows = jnp.einsum('hqk,khd->qhd', attn_probs, value_rows, precision=highest).reshape(SEQ, D)
    mixed_rows = low_back(low(mixed_rows))
    attn_out = low_back(jnp.dot(mixed_rows, out_weight, precision=highest) + out_bias)
    return one_image + attn_out

def expert_block(inputs):
    rows_in, w_in, b_in, w_out, b_out = inputs
    pre_act = low_back(jnp.dot(rows_in, w_in, precision=highest) + b_in)
    activation = low(jax.nn.gelu(pre_act))
    return low_back(low(jnp.dot(activation, w_out, precision=highest) + b_out))

def forward(target, pairs, device_count, tokens, norm1_gain, norm1_shift, qkv_weight, qv_bias, out_weight, out_bias, norm2_gain, norm2_shift, router_weight, expert_in, expert_in_bias, expert_out, expert_out_bias):
    bias_row = jnp.concatenate([qv_bias[0], jnp.zeros((D,), jnp.float32), qv_bias[1]])
    block_fn = jax.checkpoint(lambda one_image: attend(one_image, norm1_gain, norm1_shift, qkv_weight, bias_row, out_weight, out_bias))
    resid = lax.map(block_fn, tokens).reshape(IMAGES * SEQ, D)
    hidden2 = low(norm_rows(resid, norm2_gain, norm2_shift))
    logits = low_back(jnp.dot(hidden2, router_weight, precision=highest))
    router = jax.nn.softmax(logits, axis=-1)
    gate_values = jnp.take_along_axis(router, pairs, axis=1)
    routed = low_back(jnp.repeat(hidden2, 2, axis=0))
    buffer_rows = jnp.zeros((EXPERTS * device_count * CAP, D), jnp.float32).at[target].set(routed)
    buffer_rows = buffer_rows.reshape(EXPERTS, device_count * CAP, D)
    answers = lax.map(jax.checkpoint(expert_block), (buffer_rows, expert_in, expert_in_bias, expert_out, expert_out_bias))
    picked = answers.reshape(EXPERTS * device_count * CAP, D)[target].reshape(IMAGES * SEQ, 2, D)
    combined = lax.optimization_barrier(jnp.sum(gate_values[:, :, None] * picked, axis=1))
    return (resid + combined).reshape(IMAGES, SEQ, D)

def reference(tokens, route_ids, cotangent, norm1_gain, norm1_shift, qkv_weight, qv_bias, out_weight, out_bias, norm2_gain, norm2_shift, router_weight, expert_in, expert_in_bias, expert_out, expert_out_bias):
    device_count = IMAGES // IMG_DEV
    route_flat = route_ids.reshape(-1).astype(jnp.int32)
    pair_hits = (route_flat.reshape(device_count, 2 * TOK_DEV, 1) == jnp.arange(EXPERTS, dtype=jnp.int32)).astype(jnp.int32)
    earlier = jnp.cumsum(pair_hits, axis=1, dtype=jnp.int32) - pair_hits
    slot_index = lax.optimization_barrier(jnp.sum(earlier * pair_hits, axis=2, dtype=jnp.int32)).reshape(-1)
    source = jnp.repeat(jnp.arange(device_count, dtype=jnp.int32), 2 * TOK_DEV)
    target = ((route_flat * device_count + source) * CAP + slot_index).astype(jnp.int32)
    pairs = route_ids.reshape(IMAGES * SEQ, 2).astype(jnp.int32)
    result, pullback = jax.vjp(partial(forward, target, pairs, device_count), tokens.astype(jnp.float32), norm1_gain.astype(jnp.float32), norm1_shift.astype(jnp.float32), qkv_weight.astype(jnp.float32), qv_bias.astype(jnp.float32), out_weight.astype(jnp.float32), out_bias.astype(jnp.float32), norm2_gain.astype(jnp.float32), norm2_shift.astype(jnp.float32), router_weight.astype(jnp.float32), expert_in.astype(jnp.float32), expert_in_bias.astype(jnp.float32), expert_out.astype(jnp.float32), expert_out_bias.astype(jnp.float32))
    grads = pullback(cotangent.astype(jnp.float32))
    return (result.astype(jnp.bfloat16), grads[0], grads[1], grads[2], grads[3], grads[4], grads[5], grads[6], grads[7], grads[8], grads[9], grads[10], grads[11], grads[12], grads[13])
```

```python
import math

import jax
import jax.numpy as jnp
from jax import lax
from jax.sharding import PartitionSpec as P

D = 768
HEADS = 12
HEAD = 64


epsilon = 1e-06


def normalize(values):
    mean_row = jnp.mean(values, axis=-1, keepdims=True)
    centred = values - mean_row
    variance = jnp.mean(centred * centred, axis=-1, keepdims=True)
    inv_dev = lax.rsqrt(variance + epsilon)
    return (centred * inv_dev, inv_dev)


def norm_back(grad_in, normed, inv_dev, gain):
    gain_grad = jnp.sum(grad_in * normed, axis=0)
    shift_grad = jnp.sum(grad_in, axis=0)
    scaled = grad_in * gain
    first_mean = jnp.mean(scaled, axis=-1, keepdims=True)
    second_mean = jnp.mean(scaled * normed, axis=-1, keepdims=True)
    return (gain_grad, shift_grad, inv_dev * (scaled - first_mean - normed * second_mean))


def local(
    tokens,
    route_ids,
    cotangent,
    norm1_gain,
    norm1_shift,
    qkv_weight,
    qv_bias,
    out_weight,
    out_bias,
    norm2_gain,
    norm2_shift,
    router_weight,
    expert_in,
    expert_in_bias,
    expert_out,
    expert_out_bias,
):
    images = tokens.shape[0]
    length = tokens.shape[1]
    row_count = images * length
    experts = lax.axis_size("expert")
    capacity = -(-(3 * row_count // experts) // 16) * 16
    inv_root = 1.0 / math.sqrt(HEAD)
    lowtype = jnp.bfloat16
    inputs = tokens.astype(jnp.float32).reshape(row_count, D)
    normed1, inv_dev1 = normalize(inputs)
    hidden1 = (normed1 * norm1_gain + norm1_shift).astype(lowtype)
    bias_row = jnp.concatenate([qv_bias[0], jnp.zeros((D,), jnp.float32), qv_bias[1]])
    qkv_rows = (jnp.dot(hidden1, qkv_weight, preferred_element_type=jnp.float32) + bias_row).astype(
        lowtype
    )
    qkv_heads = qkv_rows.reshape(images, length, 3, HEADS, HEAD)
    query_rows = qkv_heads[:, :, 0]
    key_rows = qkv_heads[:, :, 1]
    value_rows = qkv_heads[:, :, 2]
    scores = (
        jnp.einsum("bqhd,bkhd->bhqk", query_rows, key_rows, preferred_element_type=jnp.float32)
        * inv_root
    )
    top_score = jnp.max(scores, axis=-1, keepdims=True)
    exp_scores = jnp.exp(scores - top_score)
    exp_total = jnp.sum(exp_scores, axis=-1, keepdims=True)
    attn_probs = exp_scores / exp_total
    log_total = top_score + jnp.log(exp_total)
    mixed_rows = jnp.einsum(
        "bhqk,bkhd->bqhd",
        attn_probs.astype(lowtype),
        value_rows,
        preferred_element_type=jnp.float32,
    )
    mixed_rows = mixed_rows.reshape(row_count, D).astype(lowtype)
    attn_out = jnp.dot(mixed_rows, out_weight, preferred_element_type=jnp.float32) + out_bias
    resid = inputs + attn_out
    normed2, inv_dev2 = normalize(resid)
    hidden2 = (normed2 * norm2_gain + norm2_shift).astype(lowtype)
    logits = jnp.dot(hidden2, router_weight, preferred_element_type=jnp.float32)
    router = jax.nn.softmax(logits, axis=-1)
    route_pairs = route_ids.reshape(row_count, 2)
    expert_iota = jnp.arange(experts, dtype=jnp.int32)
    hits = (route_pairs[:, :1] == expert_iota) | (route_pairs[:, 1:] == expert_iota)
    before = lax.broadcasted_iota(jnp.int32, (row_count, row_count), 0) > (
        lax.broadcasted_iota(jnp.int32, (row_count, row_count), 1)
    )
    slot_index = jnp.dot(
        before.astype(lowtype), hits.astype(lowtype), preferred_element_type=jnp.float32
    ).astype(jnp.int32)
    slot_index = jnp.where(hits, slot_index, -1)
    slot_iota = jnp.arange(capacity, dtype=jnp.int32)
    place = slot_index[:, :, None] == slot_iota
    place_low = place.astype(lowtype).reshape(row_count, experts * capacity)
    cotangent_rows = cotangent.reshape(row_count, D)
    upstream = cotangent_rows.astype(jnp.float32)
    send_rows = jnp.einsum(
        "rs,rd->sd", place_low, hidden2, preferred_element_type=jnp.float32
    ).astype(lowtype)
    send_rows = send_rows.reshape(experts, capacity, D)
    arrived = lax.all_to_all(send_rows, "expert", split_axis=0, concat_axis=0, tiled=True)
    slot_gate = jnp.sum(jnp.where(place, router[:, :, None], 0.0), axis=0).reshape(-1, 1)
    grad_send = jnp.einsum("rs,rd->sd", place_low, cotangent_rows, preferred_element_type=jnp.float32)
    grad_send = (grad_send * slot_gate).astype(lowtype).reshape(experts, capacity, D)
    grad_arrived = lax.all_to_all(grad_send, "expert", split_axis=0, concat_axis=0, tiled=True)
    place_gate = (place * router[:, :, None]).astype(lowtype)
    place_gate = place_gate.reshape(row_count, experts * capacity)
    pre_act = (
        jnp.einsum("scd,df->scf", arrived, expert_in[0], preferred_element_type=jnp.float32)
        + expert_in_bias[0]
    )
    activation = jax.nn.gelu(pre_act).astype(lowtype)
    answer = (
        jnp.einsum("scf,fd->scd", activation, expert_out[0], preferred_element_type=jnp.float32)
        + expert_out_bias[0]
    )
    delivered = (answer.astype(lowtype), arrived, pre_act)
    answer_rows = delivered[0]
    arrived = delivered[1]
    returned = lax.all_to_all(answer_rows, "expert", split_axis=0, concat_axis=0, tiled=True)
    pre_act = delivered[2]
    activation, gelu_back = jax.vjp(jax.nn.gelu, pre_act)
    activation_low = activation.astype(lowtype)
    hidden_grad = jnp.einsum(
        "scd,fd->scf", grad_arrived, expert_out[0], preferred_element_type=jnp.float32
    )
    pre_grad = gelu_back(hidden_grad)[0].astype(lowtype)
    grad_w_out = jnp.einsum(
        "scf,scd->fd", activation_low, grad_arrived, preferred_element_type=jnp.float32
    )
    grad_b_out = jnp.sum(grad_arrived, axis=(0, 1), dtype=jnp.float32)
    grad_w_in = jnp.einsum("scf,scd->fd", pre_grad, arrived, preferred_element_type=jnp.float32)
    grad_b_in = jnp.sum(pre_grad, axis=(0, 1), dtype=jnp.float32)
    row_grad = jnp.einsum(
        "scf,df->scd", pre_grad, expert_in[0], preferred_element_type=jnp.float32
    ).astype(lowtype)
    back_rows = lax.all_to_all(row_grad, "expert", split_axis=0, concat_axis=0, tiled=True)
    parts = lax.axis_size("dp")
    width = grad_w_out.shape[0] // parts
    bias_in = grad_b_in.reshape(parts, 1, width)
    bias_in = jnp.pad(bias_in, ((0, 0), (0, 0), (0, -width % D))).reshape(parts, -1, D)
    bias_out = grad_b_out.reshape(parts, 1, D // parts)
    bias_out = jnp.pad(bias_out, ((0, 0), (0, 0), (0, D - D // parts)))
    bias_rows = jnp.concatenate([bias_in, bias_out], axis=1)
    bias_rows = jnp.pad(bias_rows, ((0, 0), (0, 16 - bias_rows.shape[1]), (0, 0)))
    expert_pack = jnp.concatenate(
        [
            grad_w_out.astype(lowtype).reshape(parts, width, D),
            grad_w_in.astype(lowtype).reshape(parts, width, D),
            bias_rows.astype(lowtype),
        ],
        axis=1,
    )
    back_rows, returned, expert_pack = lax.optimization_barrier((back_rows, returned, expert_pack))
    expert_sum = lax.psum_scatter(expert_pack, "dp", scatter_dimension=0, tiled=True)
    returned = returned.reshape(experts * capacity, D)
    combined = jnp.dot(place_gate, returned, preferred_element_type=jnp.float32)
    output = (resid + combined).astype(lowtype).reshape(images, length, D)
    expert_part = jnp.dot(
        place_low, back_rows.reshape(experts * capacity, D), preferred_element_type=jnp.float32
    )
    pair_grad = jnp.einsum(
        "rd,sd->rs", cotangent_rows, returned, preferred_element_type=jnp.float32
    ).reshape(row_count, experts, capacity)
    prob_grad = jnp.sum(jnp.where(place, pair_grad, 0.0), axis=-1)
    logit_grad = router * (prob_grad - jnp.sum(router * prob_grad, axis=-1, keepdims=True))
    logit_grad = logit_grad.astype(lowtype)
    grad_router = jnp.einsum("rd,re->de", hidden2, logit_grad, preferred_element_type=jnp.float32)
    hidden2_grad = expert_part + jnp.einsum(
        "re,de->rd", logit_grad, router_weight, preferred_element_type=jnp.float32
    )
    grad_gain2, grad_shift2, norm2_input = norm_back(hidden2_grad, normed2, inv_dev2, norm2_gain)
    resid_grad = upstream + norm2_input
    attn_grad = resid_grad.astype(lowtype)
    grad_out_w = jnp.einsum("rd,re->de", mixed_rows, attn_grad, preferred_element_type=jnp.float32)
    grad_out_b = jnp.sum(attn_grad, axis=0, dtype=jnp.float32)
    mixed_grad = jnp.einsum("re,de->rd", attn_grad, out_weight, preferred_element_type=jnp.float32)
    mixed_grad = mixed_grad.astype(lowtype).reshape(images, length, HEADS, HEAD)
    scores_again = (
        jnp.einsum("bqhd,bkhd->bhqk", query_rows, key_rows, preferred_element_type=jnp.float32)
        * inv_root
    )
    probs_again = jnp.exp(scores_again - log_total)
    value_grad = jnp.einsum(
        "bhqk,bqhd->bkhd",
        probs_again.astype(lowtype),
        mixed_grad,
        preferred_element_type=jnp.float32,
    )
    weight_grad = jnp.einsum(
        "bqhd,bkhd->bhqk", mixed_grad, value_rows, preferred_element_type=jnp.float32
    )
    score_grad = probs_again * (
        weight_grad - jnp.sum(probs_again * weight_grad, axis=-1, keepdims=True)
    )
    score_grad = score_grad.astype(lowtype)
    query_grad = (
        jnp.einsum("bhqk,bkhd->bqhd", score_grad, key_rows, preferred_element_type=jnp.float32)
        * inv_root
    )
    key_grad = (
        jnp.einsum("bhqk,bqhd->bkhd", score_grad, query_rows, preferred_element_type=jnp.float32)
        * inv_root
    )
    qkv_grad = (
        jnp.stack([query_grad, key_grad, value_grad], axis=2)
        .reshape(row_count, 3 * D)
        .astype(lowtype)
    )
    grad_qkv_w = jnp.einsum("rd,rf->df", hidden1, qkv_grad, preferred_element_type=jnp.float32)
    qkv_sums = jnp.sum(qkv_grad, axis=0, dtype=jnp.float32)
    grad_qv_b = jnp.stack([qkv_sums[:D], qkv_sums[2 * D :]])
    hidden1_grad = jnp.einsum("rf,df->rd", qkv_grad, qkv_weight, preferred_element_type=jnp.float32)
    grad_gain1, grad_shift1, norm1_input = norm_back(hidden1_grad, normed1, inv_dev1, norm1_gain)
    input_grad = (resid_grad + norm1_input).reshape(images, length, D)
    small = jnp.concatenate(
        [
            grad_gain1[None],
            grad_shift1[None],
            grad_qv_b,
            grad_out_b[None],
            grad_gain2[None],
            grad_shift2[None],
            grad_router.T,
        ]
    )
    small_count = small.shape[0]
    small = jnp.pad(small, ((0, 128 - small_count), (0, 0))).T
    dense_pack = jnp.concatenate(
        [grad_qkv_w.astype(lowtype), grad_out_w.astype(lowtype), small.astype(lowtype)], axis=1
    )
    dense_total = lax.psum(dense_pack, ("dp", "expert"))
    dense_total = dense_total.astype(jnp.float32)
    small = dense_total[:, 4 * D : 4 * D + small_count].T
    expert_sum = expert_sum.astype(jnp.float32)[0]
    total_in = expert_sum[width : 2 * width].T[None]
    total_out = expert_sum[:width][None]
    bias_sum = expert_sum[2 * width :]
    in_rows = -(-width // D)
    total_b_in = bias_sum[:in_rows].reshape(1, -1)[:, :width]
    total_b_out = bias_sum[in_rows : in_rows + 1, : D // parts]
    return (
        output,
        input_grad,
        small[0],
        small[1],
        dense_total[:, : 3 * D],
        small[2:4],
        dense_total[:, 3 * D : 4 * D],
        small[4],
        small[5],
        small[6],
        small[7:].T,
        total_in,
        total_b_in,
        total_out,
        total_b_out,
    )


def solution(mesh):
    return jax.shard_map(
        local,
        mesh=mesh,
        in_specs=(
            P(("dp", "expert"), None, None),
            P(("dp", "expert"), None, None),
            P(("dp", "expert"), None, None),
            P(),
            P(),
            P(),
            P(),
            P(),
            P(),
            P(),
            P(),
            P(),
            P("expert", None, None),
            P("expert", None),
            P("expert", None, None),
            P("expert", None),
        ),
        out_specs=(
            P(("dp", "expert"), None, None),
            P(("dp", "expert"), None, None),
            P(),
            P(),
            P(),
            P(),
            P(),
            P(),
            P(),
            P(),
            P(),
            P("expert", None, "dp"),
            P("expert", "dp"),
            P("expert", "dp", None),
            P("expert", "dp"),
        ),
        check_vma=False,
    )
```
